32 devices in a mesh: pipe: 8 (over y, x, core), dp: 4 (over z).
Axes of the slice: x: 2, y: 2, z: 4, core: 2. Of those that a mesh axis runs over, the one named last changes fastest.
Arguments:
- up_input: bfloat16 [4, 256, 1536], P(None, 'dp'), may hold values from -6 to 6
- down_input: bfloat16 [4, 256, 1536], P(None, 'dp'), may hold values from -6 to 6
- up_cotangent: bfloat16 [4, 256, 1536], P(None, 'dp'), may hold values from -6 to 6
- down_cotangent: bfloat16 [4, 256, 1536], P(None, 'dp'), may hold values from -6 to 6
- weights: bfloat16 [8, 1536, 1536], P('pipe'), may hold values from -0.15625 to 0.15625
Outputs:
- section_outputs: bfloat16 [2, 8, 4, 256, 1536], P(None, 'pipe', None, 'dp')
- input_grads: bfloat16 [2, 8, 4, 256, 1536], P(None, 'pipe', None, 'dp')
- weight_grads: float32 [8, 1536, 1536], P('pipe', 'dp')
The draws below stay inside these ranges and needn't reach their ends.
All inputs are finite; a program needn't handle non-finite values.
Results may differ from the reference program's by a relative error of at most 0.015.
Values may be sent and summed in bfloat16 or wider, within the bound.
A program may use at most 128 MiB of HBM per device.

```python
import jax
import jax.numpy as jnp
from jax import lax

D = 1536
MICRO = 4
MB = 64
REPLICAS = 4
LAYERS = 8
TOKENS = 256


def level_of(rng, shape, cuts, low, largest):
    factor_of = 1.0
    for position, blocks in cuts:
        draws = jax.random.uniform(jax.random.fold_in(jax.random.fold_in(rng, 6), position), (blocks,), jnp.float32, low / len(cuts), largest / len(cuts))
        factor_of = factor_of * jnp.repeat(jnp.exp(draws), shape[position] // blocks).reshape((-1,) + (1,) * (len(shape) - 1 - position))
    return factor_of


def normal_values(own_key, shape, scale, reach, split=(), held_as=jnp.bfloat16):
    array = scale * jax.random.normal(own_key, shape, jnp.float32)
    if split:
        array = array * level_of(own_key, shape, split, -0.22, 0.18)
    return jnp.clip(array, -reach, reach).astype(held_as)


def setup_inputs(seed: int = 0) -> dict:
    key_list = jax.random.split(jax.random.key(seed), 6)
    return {
        "up_input": normal_values(key_list[0], (MICRO, TOKENS, D), 1.0, 6.0, ((1, 4),)),
        "down_input": normal_values(key_list[1], (MICRO, TOKENS, D), 1.0, 6.0, ((1, 4),)),
        "up_cotangent": normal_values(key_list[2], (MICRO, TOKENS, D), 1.0, 6.0, ((1, 4),)),
        "down_cotangent": normal_values(key_list[3], (MICRO, TOKENS, D), 1.0, 6.0, ((1, 4),)),
        "weights": normal_values(key_list[4], (LAYERS, D, D), D ** -0.5, 0.15625, ((0, 8),)),
    }


NORM_EPS = 1e-06

def forward_layer(layer_in, weight):
    inputs_f32 = layer_in.astype(jnp.float32)
    inv_rms = lax.rsqrt(lax.optimization_barrier(jnp.mean(inputs_f32 * inputs_f32, axis=-1, keepdims=True)) + NORM_EPS)
    hidden = (inputs_f32 * inv_rms).astype(jnp.bfloat16)
    pre_act = jnp.dot(hidden, weight, preferred_element_type=jnp.float32)
    layer_out = (inputs_f32 + jax.nn.silu(pre_act)).astype(jnp.bfloat16)
    return (layer_out, hidden, pre_act)

def backward_layer(layer_in, pre_act, weight, grad_out):
    inputs_f32 = layer_in.astype(jnp.float32)
    inv_rms = lax.rsqrt(lax.optimization_barrier(jnp.mean(inputs_f32 * inputs_f32, axis=-1, keepdims=True)) + NORM_EPS)
    grad_f32 = grad_out.astype(jnp.float32)
    sigmoid_pre = jax.nn.sigmoid(pre_act)
    grad_pre = (grad_f32 * sigmoid_pre * (1.0 + pre_act * (1.0 - sigmoid_pre))).astype(jnp.bfloat16)
    grad_hidden = lax.dot_general(grad_pre, weight, (((1,), (1,)), ((), ())), preferred_element_type=jnp.float32)
    inner = lax.optimization_barrier(jnp.mean(grad_hidden * inputs_f32, axis=-1, keepdims=True))
    grad_in = grad_f32 + inv_rms * (grad_hidden - inputs_f32 * inv_rms * inv_rms * inner)
    return (grad_in.astype(jnp.bfloat16), grad_pre)

def reference(up_input, down_input, up_cotangent, down_cotangent, weights):
    current = jnp.stack([up_input, down_input]).reshape(-1, D)
    layer_inputs = []
    layer_outputs = []
    for layer_id in range(LAYERS):
        layer_inputs.append(current)
        current = forward_layer(current, weights[layer_id])[0]
        layer_outputs.append(current)
    grad_flow = jnp.stack([up_cotangent, down_cotangent]).reshape(-1, D)
    input_list = [None] * LAYERS
    weight_list = [None] * LAYERS
    for layer_id in range(LAYERS - 1, -1, -1):
        layer_in = layer_inputs[layer_id]
        unused, hidden, pre_act = forward_layer(layer_in, weights[layer_id])
        grad_flow, grad_pre = backward_layer(layer_in, pre_act, weights[layer_id], grad_flow)
        input_list[layer_id] = grad_flow
        hidden_five = hidden.astype(jnp.float32).reshape(2, MICRO, REPLICAS, MB, D)
        grad_five = grad_pre.astype(jnp.float32).reshape(2, MICRO, REPLICAS, MB, D)
        partial_sums = jnp.einsum('smrtd,smrte->srde', hidden_five, grad_five)
        rounded = lax.optimization_barrier(partial_sums.astype(jnp.bfloat16))
        weight_list[layer_id] = lax.optimization_barrier(jnp.sum(rounded.astype(jnp.float32), axis=(0, 1)))
    outputs_all = jnp.stack(layer_outputs).reshape(LAYERS, 2, MICRO, TOKENS, D)
    grads_all = jnp.stack(input_list).reshape(LAYERS, 2, MICRO, TOKENS, D)
    section_outputs = jnp.stack([outputs_all[:, 0], outputs_all[::-1, 1]])
    input_grads = jnp.stack([grads_all[:, 0], grads_all[::-1, 1]])
    weight_grads = jnp.stack(weight_list)
    return (section_outputs, input_grads, weight_grads)
```

```python
import functools

import jax
import jax.numpy as jnp
from jax import lax
from jax.experimental import pallas as pl
from jax.experimental.pallas import tpu as pltpu
from jax.sharding import PartitionSpec as P

NORM_EPS = 1e-06
MESH = pl.DeviceIdType.MESH
F32 = jnp.float32
BF16 = jnp.bfloat16


def window_kernel(
    sections,
    replicas,
    up_in,
    down_in,
    up_ct,
    down_ct,
    weight,
    out,
    grads,
    wgrad,
    vin,
    y,
    hid,
    hid_t,
    slope,
    inv,
    gin,
    gp,
    gout,
    gh,
    rs_send,
    rs_recv,
    load_sem,
    fs_sem,
    fr_sem,
    bs_sem,
    br_sem,
    oms_sem,
    omr_sem,
    gms_sem,
    gmr_sem,
    rss_sem,
    rsr_sem,
):
    p = lax.axis_index("pipe")
    z = lax.axis_index("dp")
    steps, rows, width = vin.shape
    micro = steps // 2
    last = sections - 1
    after = lax.rem(p + 1, sections)
    before = lax.rem(p + sections - 1, sections)
    mirror = last - p
    z_next = lax.rem(z + 1, replicas)
    z_prev = lax.rem(z + replicas - 1, replicas)
    tile = 512 if width % 512 == 0 else width
    tiles = width // tile
    blocks = rs_send.shape[1]
    block_w = width // blocks
    chunk_rows = width // replicas

    barrier = pltpu.get_barrier_semaphore()
    for peer in ((after, z), (before, z), (mirror, z), (p, z_next), (p, z_prev)):
        pl.semaphore_signal(barrier, inc=1, device_id=peer, device_id_type=MESH)

    def load(source, target, index):
        return pltpu.make_async_copy(source, target, load_sem.at[index])

    @pl.when(p == 0)
    def _():
        load(down_in, vin.at[pl.ds(0, micro)], 0).start()
        load(up_in, vin.at[pl.ds(micro, micro)], 1).start()

    @pl.when(p == last)
    def _():
        load(down_ct, gin.at[pl.ds(0, micro)], 2).start()
        load(up_ct, gin.at[pl.ds(micro, micro)], 3).start()

    pl.semaphore_wait(barrier, 5)

    def forward_send(i, t):
        part = pl.ds(t * tile, tile)
        return pltpu.make_async_remote_copy(
            src_ref=y.at[i, :, part],
            dst_ref=vin.at[i, :, part],
            send_sem=fs_sem.at[i, t],
            recv_sem=fr_sem.at[i, t],
            device_id=(after, z),
            device_id_type=MESH,
        )

    def backward_send(i):
        return pltpu.make_async_remote_copy(
            src_ref=gout.at[i],
            dst_ref=gin.at[i],
            send_sem=bs_sem.at[i],
            recv_sem=br_sem.at[i],
            device_id=(before, z),
            device_id_type=MESH,
        )

    def mirror_send(source, target, send_sem, recv_sem, i):
        return pltpu.make_async_remote_copy(
            src_ref=source.at[i],
            dst_ref=target.at[1, i],
            send_sem=send_sem.at[i],
            recv_sem=recv_sem.at[i],
            device_id=(mirror, z),
            device_id_type=MESH,
        )

    def keep(source, target, sem, i):
        return pltpu.make_async_copy(source.at[i], target.at[0, i - micro], sem.at[i])

    @pl.when(p == 0)
    def _():
        load(down_in, vin.at[pl.ds(0, micro)], 0).wait()
        load(up_in, vin.at[pl.ds(micro, micro)], 1).wait()

    def forward(i, carry):
        @pl.when(p > 0)
        def _():
            for t in range(tiles):
                forward_send(i, t).wait_recv()

        v = vin[i].astype(F32)
        s = lax.rsqrt(jnp.mean(v * v, axis=-1, keepdims=True) + NORM_EPS)
        hidden = (v * s).astype(BF16)
        hid[i] = hidden
        inv[i] = jnp.broadcast_to(s, (rows, 128))
        for t in range(tiles):
            cols = slice(t * tile, (t + 1) * tile)
            pre = jnp.dot(hidden, weight[0, :, cols], preferred_element_type=F32)
            sigma = 1.0 / (1.0 + jnp.exp(-pre))
            y[i, :, cols] = (vin[i, :, cols].astype(F32) + pre * sigma).astype(BF16)

            @pl.when(p < last)
            def _():
                forward_send(i, t).start()

            slope[i, :, cols] = sigma * (1.0 + pre * (1.0 - sigma))

        @pl.when(i < micro)
        def _():
            mirror_send(y, out, oms_sem, omr_sem, i).start()

        @pl.when(i >= micro)
        def _():
            keep(y, out, oms_sem, i).start()

        return carry

    lax.fori_loop(0, steps, forward, 0)

    def transpose_hidden():
        per = 128 // rows
        for j in range(steps // per):
            block = hid[j * per : (j + 1) * per].reshape(per * rows, width)
            hid_t[:, j * 128 : (j + 1) * 128] = block.T

    @pl.when(p < sections // 2)
    def _():
        transpose_hidden()

    @pl.when(p == last)
    def _():
        load(down_ct, gin.at[pl.ds(0, micro)], 2).wait()
        load(up_ct, gin.at[pl.ds(micro, micro)], 3).wait()

    def backward(i, carry):
        @pl.when(p < last)
        def _():
            backward_send(i).wait_recv()

        g = gin[i].astype(F32)
        grad_pre = (g * slope[i]).astype(BF16)
        gp[i] = grad_pre
        dots = jnp.zeros((rows, 1), F32)
        for t in range(tiles):
            cols = slice(t * tile, (t + 1) * tile)
            part = lax.dot_general(
                grad_pre,
                weight[0, cols, :],
                (((1,), (1,)), ((), ())),
                preferred_element_type=F32,
            )
            gh[:, cols] = part
            dots += jnp.sum(part * vin[i, :, cols].astype(F32), axis=-1, keepdims=True)
        s = inv[i][:, :1]
        factor = s * s * (dots * (1.0 / width))
        for t in range(tiles):
            cols = slice(t * tile, (t + 1) * tile)
            v = vin[i, :, cols].astype(F32)
            gout[i, :, cols] = (
                gin[i, :, cols].astype(F32) + s * (gh[:, cols] - v * factor)
            ).astype(BF16)

        @pl.when(p > 0)
        def _():
            backward_send(i).start()

        @pl.when(i < micro)
        def _():
            mirror_send(gout, grads, gms_sem, gmr_sem, i).start()

        @pl.when(i >= micro)
        def _():
            keep(gout, grads, gms_sem, i).start()

        return carry

    lax.fori_loop(0, steps, backward, 0)

    @pl.when(p >= sections // 2)
    def _():
        transpose_hidden()

    def piece(chunk, b):
        left = hid_t[pl.ds(pl.multiple_of(chunk * chunk_rows, chunk_rows), chunk_rows), :]
        right = gp[:, :, b * block_w : (b + 1) * block_w].reshape(steps * rows, block_w)
        return jnp.dot(left, right, preferred_element_type=F32)

    order = []
    for b in range(blocks // 2):
        order += [(b, 1), (blocks // 2 + b, -1)]

    def ring_send(s, b, way):
        return pltpu.make_async_remote_copy(
            src_ref=rs_send.at[s, b],
            dst_ref=rs_recv.at[s, b],
            send_sem=rss_sem.at[s, b],
            recv_sem=rsr_sem.at[s, b],
            device_id=(p, z_next if way > 0 else z_prev),
            device_id_type=MESH,
        )

    for b, way in order:
        chunk = lax.rem(z - way + replicas, replicas)
        rs_send[0, b] = piece(chunk, b).astype(BF16)
        ring_send(0, b, way).start()

    def ring(s, carry):
        for b, way in order:
            chunk = lax.rem(z - way * (1 + s) + replicas, replicas)
            own = piece(chunk, b)
            ring_send(s - 1, b, way).wait_recv()
            rs_send[s, b] = (own + rs_recv[s - 1, b].astype(F32)).astype(BF16)
            ring_send(s, b, way).start()
        return carry

    lax.fori_loop(1, replicas - 1, ring, 0)

    for b, way in order:
        wgrad[0, :, b * block_w : (b + 1) * block_w] = piece(z, b)
    for b, way in order:
        ring_send(replicas - 2, b, way).wait_recv()
        cols = slice(b * block_w, (b + 1) * block_w)
        wgrad[0, :, cols] = wgrad[0, :, cols] + rs_recv[replicas - 2, b].astype(F32)

    def drain(i, carry):
        @pl.when(p < last)
        def _():
            for t in range(tiles):
                forward_send(i, t).wait_send()

        @pl.when(p > 0)
        def _():
            backward_send(i).wait_send()

        @pl.when(i < micro)
        def _():
            mirror_send(y, out, oms_sem, omr_sem, i).wait()
            mirror_send(gout, grads, gms_sem, gmr_sem, i).wait()

        @pl.when(i >= micro)
        def _():
            keep(y, out, oms_sem, i).wait()
            keep(gout, grads, gms_sem, i).wait()

        return carry

    lax.fori_loop(0, steps, drain, 0)

    def ring_drain(s, carry):
        for b, way in order:
            ring_send(s, b, way).wait_send()
        return carry

    lax.fori_loop(0, replicas - 1, ring_drain, 0)


def local(up_input, down_input, up_cotangent, down_cotangent, weights):
    sections = lax.axis_size("pipe")
    replicas = lax.axis_size("dp")
    micro, rows, width = up_input.shape
    steps = 2 * micro
    chunk_rows = width // replicas
    blocks = 4
    tiles = width // 512 if width % 512 == 0 else 1
    block_w = width // blocks
    acts = (steps, rows, width)
    anywhere = pl.BlockSpec(memory_space=pl.ANY)
    vmem = pl.BlockSpec(memory_space=pltpu.VMEM)
    dma = pltpu.SemaphoreType.DMA
    flops = 6 * steps * rows * width * width
    outs, grads, wgrad = pl.pallas_call(
        functools.partial(window_kernel, sections, replicas),
        out_shape=(
            jax.ShapeDtypeStruct((2, micro, rows, width), BF16),
            jax.ShapeDtypeStruct((2, micro, rows, width), BF16),
            jax.ShapeDtypeStruct((1, chunk_rows, width), F32),
        ),
        in_specs=[anywhere] * 4 + [vmem],
        out_specs=(anywhere, anywhere, vmem),
        scratch_shapes=[
            pltpu.VMEM(acts, BF16),
            pltpu.VMEM(acts, BF16),
            pltpu.VMEM(acts, BF16),
            pltpu.VMEM((width, steps * rows), BF16),
            pltpu.VMEM(acts, F32),
            pltpu.VMEM((steps, rows, 128), F32),
            pltpu.VMEM(acts, BF16),
            pltpu.VMEM(acts, BF16),
            pltpu.VMEM(acts, BF16),
            pltpu.VMEM((rows, width), F32),
            pltpu.VMEM((replicas - 1, blocks, chunk_rows, block_w), BF16),
            pltpu.VMEM((replicas - 1, blocks, chunk_rows, block_w), BF16),
            dma((4,)),
            dma((steps, tiles)),
            dma((steps, tiles)),
            dma((steps,)),
            dma((steps,)),
            dma((steps,)),
            dma((steps,)),
            dma((steps,)),
            dma((steps,)),
            dma((replicas - 1, blocks)),
            dma((replicas - 1, blocks)),
        ],
        compiler_params=pltpu.CompilerParams(
            collective_id=0, has_side_effects=True, vmem_limit_bytes=50 * 1024 * 1024
        ),
        cost_estimate=pl.CostEstimate(
            flops=flops, bytes_accessed=20 * 1024 * 1024, transcendentals=steps * rows * width
        ),
    )(up_input, down_input, up_cotangent, down_cotangent, weights)
    return (outs[:, None], grads[:, None], wgrad)


def solution(mesh):
    return jax.shard_map(
        local,
        mesh=mesh,
        in_specs=(
            P(None, "dp", None),
            P(None, "dp", None),
            P(None, "dp", None),
            P(None, "dp", None),
            P("pipe", None, None),
        ),
        out_specs=(
            P(None, "pipe", None, "dp", None),
            P(None, "pipe", None, "dp", None),
            P("pipe", "dp", None),
        ),
        check_vma=False,
    )
```

```python
import functools

import jax
import jax.numpy as jnp
from jax import lax
from jax.experimental import pallas as pl
from jax.experimental.pallas import tpu as pltpu
from jax.sharding import PartitionSpec as P

NORM_EPS = 1e-06
LEAD = 4
MESH = pl.DeviceIdType.MESH
F32 = jnp.float32
BF16 = jnp.bfloat16


def window_kernel(
    sections,
    replicas,
    up_in,
    down_in,
    up_ct,
    down_ct,
    weight_hbm,
    out,
    grads,
    wgrad,
    weight,
    weight_t,
    vin,
    y,
    hid,
    hid_t,
    slope,
    inv,
    gin,
    gp,
    gout,
    gh,
    rs_send,
    rs_recv,
    load_sem,
    fs_sem,
    fr_sem,
    bs_sem,
    br_sem,
    oms_sem,
    omr_sem,
    gms_sem,
    gmr_sem,
    rss_sem,
    rsr_sem,
):
    p = lax.axis_index("pipe")
    z = lax.axis_index("dp")
    steps, rows, width = vin.shape
    micro = steps // 2
    last = sections - 1
    after = lax.rem(p + 1, sections)
    before = lax.rem(p + sections - 1, sections)
    mirror = last - p
    z_next = lax.rem(z + 1, replicas)
    z_prev = lax.rem(z + replicas - 1, replicas)
    tile = 512 if width % 512 == 0 else width
    tiles = width // tile
    blocks = rs_send.shape[1]
    block_w = width // blocks
    chunk_rows = width // replicas

    barrier = pltpu.get_barrier_semaphore()
    for peer in ((after, z), (before, z), (mirror, z), (p, z_next), (p, z_prev)):
        pl.semaphore_signal(barrier, inc=1, device_id=peer, device_id_type=MESH)

    def load(source, target, index):
        return pltpu.make_async_copy(source, target, load_sem.at[index])

    load(weight_hbm.at[0], weight, 4).start()

    @pl.when(p == 0)
    def _():
        load(down_in, vin.at[pl.ds(0, micro)], 0).start()
        load(up_in, vin.at[pl.ds(micro, micro)], 1).start()

    @pl.when(p == last)
    def _():
        load(down_ct, gin.at[pl.ds(0, micro)], 2).start()
        load(up_ct, gin.at[pl.ds(micro, micro)], 3).start()

    def forward_send(i, t):
        part = pl.ds(t * tile, tile)
        return pltpu.make_async_remote_copy(
            src_ref=y.at[i, :, part],
            dst_ref=vin.at[i, :, part],
            send_sem=fs_sem.at[i, t],
            recv_sem=fr_sem.at[i, t],
            device_id=(after, z),
            device_id_type=MESH,
        )

    def backward_send(i):
        return pltpu.make_async_remote_copy(
            src_ref=gout.at[i],
            dst_ref=gin.at[i],
            send_sem=bs_sem.at[i],
            recv_sem=br_sem.at[i],
            device_id=(before, z),
            device_id_type=MESH,
        )

    def mirror_send(source, target, send_sem, recv_sem, i):
        return pltpu.make_async_remote_copy(
            src_ref=source.at[i],
            dst_ref=target.at[1, i],
            send_sem=send_sem.at[i],
            recv_sem=recv_sem.at[i],
            device_id=(mirror, z),
            device_id_type=MESH,
        )

    def keep(source, target, sem, i):
        return pltpu.make_async_copy(source.at[i], target.at[0, i - micro], sem.at[i])

    @pl.when(p == 0)
    def _():
        load(down_in, vin.at[pl.ds(0, micro)], 0).wait()
        load(up_in, vin.at[pl.ds(micro, micro)], 1).wait()

    load(weight_hbm.at[0], weight, 4).wait()
    pl.semaphore_wait(barrier, 5)

    def transpose_weight():
        def strip(j, carry):
            rows_of = pl.ds(pl.multiple_of(j * 128, 128), 128)
            for k in range(width // 256):
                cols = slice(k * 256, (k + 1) * 256)
                weight_t[cols, rows_of] = weight[rows_of, cols].T
            return carry

        lax.fori_loop(0, width // 128, strip, 0)

    @pl.when(p >= sections // 2)
    def _():
        transpose_weight()

    def forward(i):
        @pl.when(p > 0)
        def _():
            for t in range(tiles):
                forward_send(i, t).wait_recv()

        v = vin[i].astype(F32)
        s = lax.rsqrt(jnp.mean(v * v, axis=-1, keepdims=True) + NORM_EPS)
        hidden = (v * s).astype(BF16)
        hid[i] = hidden
        inv[i] = jnp.broadcast_to(s, (rows, 128))
        for t in range(tiles):
            cols = slice(t * tile, (t + 1) * tile)
            pre = jnp.dot(hidden, weight[:, cols], preferred_element_type=F32)
            sigma = 1.0 / (1.0 + jnp.exp(-pre))
            y[i, :, cols] = (vin[i, :, cols].astype(F32) + pre * sigma).astype(BF16)

            @pl.when(p < last)
            def _():
                forward_send(i, t).start()

            slope[i, :, cols] = sigma * (1.0 + pre * (1.0 - sigma))

        @pl.when(i >= micro)
        def _():
            keep(y, out, oms_sem, i).start()

    def transpose_hidden():
        per = 128 // rows
        for j in range(steps // per):
            block = hid[j * per : (j + 1) * per].reshape(per * rows, width)
            hid_t[:, j * 128 : (j + 1) * 128] = block.T

    @pl.when(p == last)
    def _():
        load(down_ct, gin.at[pl.ds(0, micro)], 2).wait()
        load(up_ct, gin.at[pl.ds(micro, micro)], 3).wait()

    def backward(i):
        @pl.when(p < last)
        def _():
            backward_send(i).wait_recv()

        g = gin[i].astype(F32)
        grad_pre = (g * slope[i]).astype(BF16)
        gp[i] = grad_pre
        dots = jnp.zeros((rows, 1), F32)
        for t in range(tiles):
            cols = slice(t * tile, (t + 1) * tile)
            part = jnp.dot(grad_pre, weight_t[:, cols], preferred_element_type=F32)
            gh[:, cols] = part
            dots += jnp.sum(part * vin[i, :, cols].astype(F32), axis=-1, keepdims=True)
        s = inv[i][:, :1]
        factor = s * s * (dots * (1.0 / width))
        for t in range(tiles):
            cols = slice(t * tile, (t + 1) * tile)
            v = vin[i, :, cols].astype(F32)
            gout[i, :, cols] = (
                gin[i, :, cols].astype(F32) + s * (gh[:, cols] - v * factor)
            ).astype(BF16)

        @pl.when(p > 0)
        def _():
            backward_send(i).start()

        @pl.when(i >= micro)
        def _():
            keep(gout, grads, gms_sem, i).start()

    lead = jnp.minimum(steps, LEAD * (last - p))

    def turn(t, carry):
        @pl.when(t < steps)
        def _():
            forward(t)

        @pl.when(t == steps - 1)
        def _():
            transpose_hidden()

            @pl.when(p < sections // 2)
            def _():
                transpose_weight()


        @pl.when(t >= lead)
        def _():
            backward(t - lead)

        return carry

    lax.fori_loop(0, steps + lead, turn, 0)

    def piece(chunk, b):
        left = hid_t[pl.ds(pl.multiple_of(chunk * chunk_rows, chunk_rows), chunk_rows), :]
        right = gp[:, :, b * block_w : (b + 1) * block_w].reshape(steps * rows, block_w)
        return jnp.dot(left, right, preferred_element_type=F32)

    order = []
    for b in range(blocks // 2):
        order += [(b, 1), (blocks // 2 + b, -1)]

    def ring_send(s, b, way):
        return pltpu.make_async_remote_copy(
            src_ref=rs_send.at[s, b],
            dst_ref=rs_recv.at[s, b],
            send_sem=rss_sem.at[s, b],
            recv_sem=rsr_sem.at[s, b],
            device_id=(p, z_next if way > 0 else z_prev),
            device_id_type=MESH,
        )

    for b, way in order:
        chunk = lax.rem(z - way + replicas, replicas)
        rs_send[0, b] = piece(chunk, b).astype(BF16)
        ring_send(0, b, way).start()

    def to_mirror(i, carry):
        mirror_send(y, out, oms_sem, omr_sem, i).start()
        mirror_send(gout, grads, gms_sem, gmr_sem, i).start()
        return carry

    lax.fori_loop(0, micro, to_mirror, 0)

    def ring(s, carry):
        for b, way in order:
            chunk = lax.rem(z - way * (1 + s) + replicas, replicas)
            own = piece(chunk, b)
            ring_send(s - 1, b, way).wait_recv()
            rs_send[s, b] = (own + rs_recv[s - 1, b].astype(F32)).astype(BF16)
            ring_send(s, b, way).start()
        return carry

    lax.fori_loop(1, replicas - 1, ring, 0)

    for b, way in order:
        wgrad[0, :, b * block_w : (b + 1) * block_w] = piece(z, b)
    for b, way in order:
        ring_send(replicas - 2, b, way).wait_recv()
        cols = slice(b * block_w, (b + 1) * block_w)
        wgrad[0, :, cols] = wgrad[0, :, cols] + rs_recv[replicas - 2, b].astype(F32)

    def drain(i, carry):
        @pl.when(p < last)
        def _():
            for t in range(tiles):
                forward_send(i, t).wait_send()

        @pl.when(p > 0)
        def _():
            backward_send(i).wait_send()

        @pl.when(i < micro)
        def _():
            mirror_send(y, out, oms_sem, omr_sem, i).wait()
            mirror_send(gout, grads, gms_sem, gmr_sem, i).wait()

        @pl.when(i >= micro)
        def _():
            keep(y, out, oms_sem, i).wait()
            keep(gout, grads, gms_sem, i).wait()

        return carry

    lax.fori_loop(0, steps, drain, 0)

    def ring_drain(s, carry):
        for b, way in order:
            ring_send(s, b, way).wait_send()
        return carry

    lax.fori_loop(0, replicas - 1, ring_drain, 0)


def local(up_input, down_input, up_cotangent, down_cotangent, weights):
    sections = lax.axis_size("pipe")
    replicas = lax.axis_size("dp")
    micro, rows, width = up_input.shape
    steps = 2 * micro
    chunk_rows = width // replicas
    blocks = 4
    tiles = width // 512 if width % 512 == 0 else 1
    block_w = width // blocks
    acts = (steps, rows, width)
    anywhere = pl.BlockSpec(memory_space=pltpu.HBM)
    vmem = pl.BlockSpec(memory_space=pltpu.VMEM)
    dma = pltpu.SemaphoreType.DMA
    flops = 6 * steps * rows * width * width
    outs, grads, wgrad = pl.pallas_call(
        functools.partial(window_kernel, sections, replicas),
        out_shape=(
            jax.ShapeDtypeStruct((2, micro, rows, width), BF16),
            jax.ShapeDtypeStruct((2, micro, rows, width), BF16),
            jax.ShapeDtypeStruct((1, chunk_rows, width), F32),
        ),
        in_specs=[anywhere] * 5,
        out_specs=(anywhere, anywhere, vmem),
        scratch_shapes=[
            pltpu.VMEM((width, width), BF16),
            pltpu.VMEM((width, width), BF16),
            pltpu.VMEM(acts, BF16),
            pltpu.VMEM(acts, BF16),
            pltpu.VMEM(acts, BF16),
            pltpu.VMEM((width, steps * rows), BF16),
            pltpu.VMEM(acts, F32),
            pltpu.VMEM((steps, rows, 128), F32),
            pltpu.VMEM(acts, BF16),
            pltpu.VMEM(acts, BF16),
            pltpu.VMEM(acts, BF16),
            pltpu.VMEM((rows, width), F32),
            pltpu.VMEM((replicas - 1, blocks, chunk_rows, block_w), BF16),
            pltpu.VMEM((replicas - 1, blocks, chunk_rows, block_w), BF16),
            dma((5,)),
            dma((steps, tiles)),
            dma((steps, tiles)),
            dma((steps,)),
            dma((steps,)),
            dma((steps,)),
            dma((steps,)),
            dma((steps,)),
            dma((steps,)),
            dma((replicas - 1, blocks)),
            dma((replicas - 1, blocks)),
        ],
        compiler_params=pltpu.CompilerParams(
            collective_id=0, has_side_effects=True, vmem_limit_bytes=50 * 1024 * 1024
        ),
        cost_estimate=pl.CostEstimate(
            flops=flops, bytes_accessed=20 * 1024 * 1024, transcendentals=steps * rows * width
        ),
    )(up_input, down_input, up_cotangent, down_cotangent, weights)
    return (outs[:, None], grads[:, None], wgrad)


def solution(mesh):
    return jax.shard_map(
        local,
        mesh=mesh,
        in_specs=(
            P(None, "dp", None),
            P(None, "dp", None),
            P(None, "dp", None),
            P(None, "dp", None),
            P("pipe", None, None),
        ),
        out_specs=(
            P(None, "pipe", None, "dp", None),
            P(None, "pipe", None, "dp", None),
            P("pipe", "dp", None),
        ),
        check_vma=False,
    )
```

```python
import functools

import jax
import jax.numpy as jnp
from jax import lax
from jax.experimental import pallas as pl
from jax.experimental.pallas import tpu as pltpu
from jax.sharding import PartitionSpec as P

NORM_EPS = 1e-06
LEAD = 4
MESH = pl.DeviceIdType.MESH
F32 = jnp.float32
BF16 = jnp.bfloat16


def window_kernel(
    sections,
    replicas,
    up_in,
    down_in,
    up_ct,
    down_ct,
    weight_hbm,
    out,
    grads,
    wgrad,
    weight,
    weight_t,
    vin,
    y,
    hid,
    hid_t,
    slope,
    inv,
    gin,
    gp,
    gout,
    gh,
    rs_send,
    rs_recv,
    tail_send,
    tail_recv,
    pair_hid,
    pair_gp,
    load_sem,
    fs_sem,
    fr_sem,
    bs_sem,
    br_sem,
    oms_sem,
    omr_sem,
    gms_sem,
    gmr_sem,
    rss_sem,
    rsr_sem,
    ts_sem,
    tr_sem,
    phs_sem,
    phr_sem,
    pgs_sem,
    pgr_sem,
    pbs_sem,
    pbr_sem,
):
    p = lax.axis_index("pipe")
    z = lax.axis_index("dp")
    steps, rows, width = vin.shape
    micro = steps // 2
    last = sections - 1
    after = lax.rem(p + 1, sections)
    before = lax.rem(p + sections - 1, sections)
    mirror = last - p
    z_next = lax.rem(z + 1, replicas)
    z_prev = lax.rem(z + replicas - 1, replicas)
    tile = 512 if width % 512 == 0 else width
    tiles = width // tile
    blocks = rs_send.shape[1]
    block_w = width // blocks
    chunk_rows = width // replicas

    barrier = pltpu.get_barrier_semaphore()
    for peer in ((after, z), (before, z), (mirror, z), (p, z_next), (p, z_prev)):
        pl.semaphore_signal(barrier, inc=1, device_id=peer, device_id_type=MESH)

    def load(source, target, index):
        return pltpu.make_async_copy(source, target, load_sem.at[index])

    load(weight_hbm.at[0], weight, 4).start()

    @pl.when(p == 0)
    def _():
        load(down_in, vin.at[pl.ds(0, micro)], 0).start()
        load(up_in, vin.at[pl.ds(micro, micro)], 1).start()

    @pl.when(p == last)
    def _():
        load(down_ct, gin.at[pl.ds(0, micro)], 2).start()
        load(up_ct, gin.at[pl.ds(micro, micro)], 3).start()

    def forward_send(i, t):
        part = pl.ds(t * tile, tile)
        return pltpu.make_async_remote_copy(
            src_ref=y.at[i, :, part],
            dst_ref=vin.at[i, :, part],
            send_sem=fs_sem.at[i, t],
            recv_sem=fr_sem.at[i, t],
            device_id=(after, z),
            device_id_type=MESH,
        )

    def backward_send(i):
        return pltpu.make_async_remote_copy(
            src_ref=gout.at[i],
            dst_ref=gin.at[i],
            send_sem=bs_sem.at[i],
            recv_sem=br_sem.at[i],
            device_id=(before, z),
            device_id_type=MESH,
        )

    def mirror_send(source, target, send_sem, recv_sem, i):
        return pltpu.make_async_remote_copy(
            src_ref=source.at[i],
            dst_ref=target.at[1, i],
            send_sem=send_sem.at[i],
            recv_sem=recv_sem.at[i],
            device_id=(mirror, z),
            device_id_type=MESH,
        )

    line = replicas == 4
    eager = steps // 2
    is_end = jnp.logical_or(z == 0, z == replicas - 1)
    pair = z + 1 - 2 * lax.rem(z, 2)
    middle = jnp.where(z == 1, 2, 1)
    far = jnp.where(z == 1, 3, 0)
    kept = width - chunk_rows

    def pair_hid_send():
        part = pl.ds(pl.multiple_of(jnp.where(z == 0, chunk_rows, 0), chunk_rows), kept)
        return pltpu.make_async_remote_copy(
            src_ref=hid_t.at[part],
            dst_ref=pair_hid.at[part],
            send_sem=phs_sem.at[0],
            recv_sem=phr_sem.at[0],
            device_id=(p, pair),
            device_id_type=MESH,
        )

    def pair_gp_send(i):
        return pltpu.make_async_remote_copy(
            src_ref=gp.at[i],
            dst_ref=pair_gp.at[i],
            send_sem=pgs_sem.at[i],
            recv_sem=pgr_sem.at[i],
            device_id=(p, pair),
            device_id_type=MESH,
        )

    def pair_block_send(j):
        part = (pl.ds(eager, steps - eager), slice(None), pl.ds(j * block_w, block_w))
        return pltpu.make_async_remote_copy(
            src_ref=gp.at[part],
            dst_ref=pair_gp.at[part],
            send_sem=pbs_sem.at[j],
            recv_sem=pbr_sem.at[j],
            device_id=(p, pair),
            device_id_type=MESH,
        )

    def middle_copy(k, j):
        return pltpu.make_async_remote_copy(
            src_ref=rs_send.at[k, j],
            dst_ref=rs_recv.at[k, j],
            send_sem=rss_sem.at[k, j],
            recv_sem=rsr_sem.at[k, j],
            device_id=(p, middle),
            device_id_type=MESH,
        )

    def tail_copy(j):
        return pltpu.make_async_remote_copy(
            src_ref=tail_send.at[j],
            dst_ref=tail_recv.at[j],
            send_sem=ts_sem.at[j],
            recv_sem=tr_sem.at[j],
            device_id=(p, pair),
            device_id_type=MESH,
        )

    def keep(source, target, sem, i):
        return pltpu.make_async_copy(source.at[i], target.at[0, i - micro], sem.at[i])

    @pl.when(p == 0)
    def _():
        load(down_in, vin.at[pl.ds(0, micro)], 0).wait()
        load(up_in, vin.at[pl.ds(micro, micro)], 1).wait()

    load(weight_hbm.at[0], weight, 4).wait()
    pl.semaphore_wait(barrier, 5)

    def transpose_weight():
        def strip(j, carry):
            rows_of = pl.ds(pl.multiple_of(j * 128, 128), 128)
            for k in range(width // 256):
                cols = slice(k * 256, (k + 1) * 256)
                weight_t[cols, rows_of] = weight[rows_of, cols].T
            return carry

        lax.fori_loop(0, width // 128, strip, 0)

    @pl.when(p >= sections // 2)
    def _():
        transpose_weight()

    def forward(i):
        @pl.when(p > 0)
        def _():
            for t in range(tiles):
                forward_send(i, t).wait_recv()

        v = vin[i].astype(F32)
        s = lax.rsqrt(jnp.mean(v * v, axis=-1, keepdims=True) + NORM_EPS)
        hidden = (v * s).astype(BF16)
        hid[i] = hidden
        inv[i] = jnp.broadcast_to(s, (rows, 128))
        for t in range(tiles):
            cols = slice(t * tile, (t + 1) * tile)
            pre = jnp.dot(hidden, weight[:, cols], preferred_element_type=F32)
            sigma = 1.0 / (1.0 + jnp.exp(-pre))
            y[i, :, cols] = (vin[i, :, cols].astype(F32) + pre * sigma).astype(BF16)

            @pl.when(p < last)
            def _():
                forward_send(i, t).start()

            slope[i, :, cols] = sigma * (1.0 + pre * (1.0 - sigma))

        @pl.when(i >= micro)
        def _():
            keep(y, out, oms_sem, i).start()

    def transpose_hidden():
        per = 128 // rows
        for j in range(steps // per):
            block = hid[j * per : (j + 1) * per].reshape(per * rows, width)
            hid_t[:, j * 128 : (j + 1) * 128] = block.T

    @pl.when(p == last)
    def _():
        load(down_ct, gin.at[pl.ds(0, micro)], 2).wait()
        load(up_ct, gin.at[pl.ds(micro, micro)], 3).wait()

    def backward(i):
        @pl.when(p < last)
        def _():
            backward_send(i).wait_recv()

        g = gin[i].astype(F32)
        grad_pre = (g * slope[i]).astype(BF16)
        gp[i] = grad_pre
        if line:

            @pl.when(jnp.logical_and(is_end, i < eager))
            def _():
                pair_gp_send(i).start()

        dots = jnp.zeros((rows, 1), F32)
        for t in range(tiles):
            cols = slice(t * tile, (t + 1) * tile)
            part = jnp.dot(grad_pre, weight_t[:, cols], preferred_element_type=F32)
            gh[:, cols] = part
            dots += jnp.sum(part * vin[i, :, cols].astype(F32), axis=-1, keepdims=True)
        s = inv[i][:, :1]
        factor = s * s * (dots * (1.0 / width))
        for t in range(tiles):
            cols = slice(t * tile, (t + 1) * tile)
            v = vin[i, :, cols].astype(F32)
            gout[i, :, cols] = (
                gin[i, :, cols].astype(F32) + s * (gh[:, cols] - v * factor)
            ).astype(BF16)

        @pl.when(p > 0)
        def _():
            backward_send(i).start()

        @pl.when(i >= micro)
        def _():
            keep(gout, grads, gms_sem, i).start()

    lead = jnp.minimum(steps, LEAD * (last - p))

    def turn(t, carry):
        @pl.when(t < steps)
        def _():
            forward(t)

        @pl.when(t == steps - 1)
        def _():
            transpose_hidden()
            if line:

                @pl.when(is_end)
                def _():
                    pair_hid_send().start()

            @pl.when(p < sections // 2)
            def _():
                transpose_weight()


        @pl.when(t >= lead)
        def _():
            backward(t - lead)

        return carry

    lax.fori_loop(0, steps + lead, turn, 0)

    def piece(left, right, chunk, j):
        at = pl.multiple_of(chunk * chunk_rows, chunk_rows)
        return jnp.dot(
            left[pl.ds(at, chunk_rows), :],
            right[:, :, j * block_w : (j + 1) * block_w].reshape(steps * rows, block_w),
            preferred_element_type=F32,
        )

    def to_mirror(i, carry):
        mirror_send(y, out, oms_sem, omr_sem, i).start()
        mirror_send(gout, grads, gms_sem, gmr_sem, i).start()
        return carry

    if line:

        @pl.when(is_end)
        def _():
            for j in range(blocks):
                pair_block_send(j).start()
            lax.fori_loop(0, micro, to_mirror, 0)
            for j in range(blocks):
                cols = slice(j * block_w, (j + 1) * block_w)
                own = piece(hid_t, gp, z, j)
                tail_copy(j).wait_recv()
                wgrad[0, :, cols] = own + tail_recv[j].astype(F32)

        @pl.when(jnp.logical_not(is_end))
        def _():
            pair_hid_send().wait_recv()
            for i in range(eager):
                pair_gp_send(i).wait_recv()
            for j in range(blocks):
                pair_block_send(j).wait_recv()
                for k, chunk in enumerate((far, middle)):
                    total = piece(hid_t, gp, chunk, j) + piece(pair_hid, pair_gp, chunk, j)
                    rs_send[k, j] = total.astype(BF16)
                    middle_copy(k, j).start()
            lax.fori_loop(0, micro, to_mirror, 0)
            for j in range(blocks):
                cols = slice(j * block_w, (j + 1) * block_w)
                own = piece(hid_t, gp, pair, j)
                middle_copy(0, j).wait_recv()
                tail_send[j] = (own + rs_recv[0, j].astype(F32)).astype(BF16)
                tail_copy(j).start()
                own = piece(hid_t, gp, z, j) + piece(pair_hid, pair_gp, z, j)
                middle_copy(1, j).wait_recv()
                wgrad[0, :, cols] = own + rs_recv[1, j].astype(F32)

    else:

        def ring_send(s, j, way):
            return pltpu.make_async_remote_copy(
                src_ref=rs_send.at[s, j],
                dst_ref=rs_recv.at[s, j],
                send_sem=rss_sem.at[s, j],
                recv_sem=rsr_sem.at[s, j],
                device_id=(p, z_next if way > 0 else z_prev),
                device_id_type=MESH,
            )

        order = []
        for j in range(blocks // 2):
            order += [(j, 1), (blocks // 2 + j, -1)]

        for j, way in order:
            chunk = lax.rem(z - way + replicas, replicas)
            rs_send[0, j] = piece(hid_t, gp, chunk, j).astype(BF16)
            ring_send(0, j, way).start()

        lax.fori_loop(0, micro, to_mirror, 0)

        def ring(s, carry):
            for j, way in order:
                chunk = lax.rem(z - way * (1 + s) + replicas, replicas)
                own = piece(hid_t, gp, chunk, j)
                ring_send(s - 1, j, way).wait_recv()
                rs_send[s, j] = (own + rs_recv[s - 1, j].astype(F32)).astype(BF16)
                ring_send(s, j, way).start()
            return carry

        lax.fori_loop(1, replicas - 1, ring, 0)

        for j, way in order:
            cols = slice(j * block_w, (j + 1) * block_w)
            own = piece(hid_t, gp, z, j)
            ring_send(replicas - 2, j, way).wait_recv()
            wgrad[0, :, cols] = own + rs_recv[replicas - 2, j].astype(F32)

    def drain(i, carry):
        @pl.when(p < last)
        def _():
            for t in range(tiles):
                forward_send(i, t).wait_send()

        @pl.when(p > 0)
        def _():
            backward_send(i).wait_send()

        @pl.when(i < micro)
        def _():
            mirror_send(y, out, oms_sem, omr_sem, i).wait()
            mirror_send(gout, grads, gms_sem, gmr_sem, i).wait()

        @pl.when(i >= micro)
        def _():
            keep(y, out, oms_sem, i).wait()
            keep(gout, grads, gms_sem, i).wait()

        return carry

    lax.fori_loop(0, steps, drain, 0)

    if line:

        @pl.when(is_end)
        def _():
            pair_hid_send().wait_send()
            for i in range(eager):
                pair_gp_send(i).wait_send()
            for j in range(blocks):
                pair_block_send(j).wait_send()

        @pl.when(jnp.logical_not(is_end))
        def _():
            for j in range(blocks):
                middle_copy(0, j).wait_send()
                middle_copy(1, j).wait_send()
                tail_copy(j).wait_send()

    else:

        def ring_drain(s, carry):
            for j, way in order:
                ring_send(s, j, way).wait_send()
            return carry

        lax.fori_loop(0, replicas - 1, ring_drain, 0)


def local(up_input, down_input, up_cotangent, down_cotangent, weights):
    sections = lax.axis_size("pipe")
    replicas = lax.axis_size("dp")
    micro, rows, width = up_input.shape
    steps = 2 * micro
    chunk_rows = width // replicas
    line = replicas == 4
    blocks = 6 if line and width % 768 == 0 else 4
    hops = 2 if line else replicas - 1
    tiles = width // 512 if width % 512 == 0 else 1
    block_w = width // blocks
    acts = (steps, rows, width)
    anywhere = pl.BlockSpec(memory_space=pltpu.HBM)
    vmem = pl.BlockSpec(memory_space=pltpu.VMEM)
    dma = pltpu.SemaphoreType.DMA
    flops = 6 * steps * rows * width * width
    outs, grads, wgrad = pl.pallas_call(
        functools.partial(window_kernel, sections, replicas),
        out_shape=(
            jax.ShapeDtypeStruct((2, micro, rows, width), BF16),
            jax.ShapeDtypeStruct((2, micro, rows, width), BF16),
            jax.ShapeDtypeStruct((1, chunk_rows, width), F32),
        ),
        in_specs=[anywhere] * 5,
        out_specs=(anywhere, anywhere, vmem),
        scratch_shapes=[
            pltpu.VMEM((width, width), BF16),
            pltpu.VMEM((width, width), BF16),
            pltpu.VMEM(acts, BF16),
            pltpu.VMEM(acts, BF16),
            pltpu.VMEM(acts, BF16),
            pltpu.VMEM((width, steps * rows), BF16),
            pltpu.VMEM(acts, F32),
            pltpu.VMEM((steps, rows, 128), F32),
            pltpu.VMEM(acts, BF16),
            pltpu.VMEM(acts, BF16),
            pltpu.VMEM(acts, BF16),
            pltpu.VMEM((rows, width), F32),
            pltpu.VMEM((hops, blocks, chunk_rows, block_w), BF16),
            pltpu.VMEM((hops, blocks, chunk_rows, block_w), BF16),
            pltpu.VMEM((blocks, chunk_rows, block_w), BF16),
            pltpu.VMEM((blocks, chunk_rows, block_w), BF16),
            pltpu.VMEM((width, steps * rows), BF16),
            pltpu.VMEM(acts, BF16),
            dma((5,)),
            dma((steps, tiles)),
            dma((steps, tiles)),
            dma((steps,)),
            dma((steps,)),
            dma((steps,)),
            dma((steps,)),
            dma((steps,)),
            dma((steps,)),
            dma((hops, blocks)),
            dma((hops, blocks)),
            dma((blocks,)),
            dma((blocks,)),
            dma((1,)),
            dma((1,)),
            dma((steps,)),
            dma((steps,)),
            dma((blocks,)),
            dma((blocks,)),
        ],
        compiler_params=pltpu.CompilerParams(
            collective_id=0, has_side_effects=True, vmem_limit_bytes=50 * 1024 * 1024
        ),
        cost_estimate=pl.CostEstimate(
            flops=flops, bytes_accessed=20 * 1024 * 1024, transcendentals=steps * rows * width
        ),
    )(up_input, down_input, up_cotangent, down_cotangent, weights)
    return (outs[:, None], grads[:, None], wgrad)


def solution(mesh):
    return jax.shard_map(
        local,
        mesh=mesh,
        in_specs=(
            P(None, "dp", None),
            P(None, "dp", None),
            P(None, "dp", None),
            P(None, "dp", None),
            P("pipe", None, None),
        ),
        out_specs=(
            P(None, "pipe", None, "dp", None),
            P(None, "pipe", None, "dp", None),
            P("pipe", "dp", None),
        ),
        check_vma=False,
    )
```

```python
import functools

import jax
import jax.numpy as jnp
from jax import lax
from jax.experimental import pallas as pl
from jax.experimental.pallas import tpu as pltpu
from jax.sharding import PartitionSpec as P

NORM_EPS = 1e-06
LEAD = 4
MESH = pl.DeviceIdType.MESH
F32 = jnp.float32
BF16 = jnp.bfloat16


def window_kernel(
    sections,
    replicas,
    up_in,
    down_in,
    up_ct,
    down_ct,
    weight_hbm,
    out,
    grads,
    wgrad,
    weight,
    weight_t,
    vin,
    y,
    hid,
    hid_t,
    slope,
    inv,
    gin,
    gp,
    gout,
    gh,
    rs_send,
    rs_recv,
    tail_send,
    tail_recv,
    pair_hid,
    pair_gp,
    load_sem,
    fs_sem,
    fr_sem,
    bs_sem,
    br_sem,
    oms_sem,
    omr_sem,
    gms_sem,
    gmr_sem,
    rss_sem,
    rsr_sem,
    ts_sem,
    tr_sem,
    phs_sem,
    phr_sem,
    pgs_sem,
    pgr_sem,
    pbs_sem,
    pbr_sem,
):
    p = lax.axis_index("pipe")
    z = lax.axis_index("dp")
    steps, rows, width = vin.shape
    micro = steps // 2
    last = sections - 1
    after = lax.rem(p + 1, sections)
    before = lax.rem(p + sections - 1, sections)
    mirror = last - p
    z_next = lax.rem(z + 1, replicas)
    z_prev = lax.rem(z + replicas - 1, replicas)
    tile = 512 if width % 512 == 0 else width
    tiles = width // tile
    blocks = rs_send.shape[1]
    block_w = width // blocks
    chunk_rows = width // replicas

    barrier = pltpu.get_barrier_semaphore()
    for peer in ((after, z), (before, z), (mirror, z), (p, z_next), (p, z_prev)):
        pl.semaphore_signal(barrier, inc=1, device_id=peer, device_id_type=MESH)

    def load(source, target, index):
        return pltpu.make_async_copy(source, target, load_sem.at[index])

    load(weight_hbm.at[0], weight, 4).start()

    @pl.when(p == 0)
    def _():
        load(down_in, vin.at[pl.ds(0, micro)], 0).start()
        load(up_in, vin.at[pl.ds(micro, micro)], 1).start()

    @pl.when(p == last)
    def _():
        load(down_ct, gin.at[pl.ds(0, micro)], 2).start()
        load(up_ct, gin.at[pl.ds(micro, micro)], 3).start()

    def forward_send(i, t):
        part = pl.ds(t * tile, tile)
        return pltpu.make_async_remote_copy(
            src_ref=y.at[i, :, part],
            dst_ref=vin.at[i, :, part],
            send_sem=fs_sem.at[i, t],
            recv_sem=fr_sem.at[i, t],
            device_id=(after, z),
            device_id_type=MESH,
        )

    def backward_send(i):
        return pltpu.make_async_remote_copy(
            src_ref=gout.at[i],
            dst_ref=gin.at[i],
            send_sem=bs_sem.at[i],
            recv_sem=br_sem.at[i],
            device_id=(before, z),
            device_id_type=MESH,
        )

    def mirror_send(source, target, send_sem, recv_sem, i):
        return pltpu.make_async_remote_copy(
            src_ref=source.at[i],
            dst_ref=target.at[1, i],
            send_sem=send_sem.at[i],
            recv_sem=recv_sem.at[i],
            device_id=(mirror, z),
            device_id_type=MESH,
        )

    line = replicas == 4
    eager = steps // 2
    is_end = jnp.logical_or(z == 0, z == replicas - 1)
    pair = z + 1 - 2 * lax.rem(z, 2)
    middle = jnp.where(z == 1, 2, 1)
    far = jnp.where(z == 1, 3, 0)
    kept = width - chunk_rows

    def pair_hid_send():
        part = pl.ds(pl.multiple_of(jnp.where(z == 0, chunk_rows, 0), chunk_rows), kept)
        return pltpu.make_async_remote_copy(
            src_ref=hid_t.at[part],
            dst_ref=pair_hid.at[part],
            send_sem=phs_sem.at[0],
            recv_sem=phr_sem.at[0],
            device_id=(p, pair),
            device_id_type=MESH,
        )

    def pair_gp_send(i):
        return pltpu.make_async_remote_copy(
            src_ref=gp.at[i],
            dst_ref=pair_gp.at[i],
            send_sem=pgs_sem.at[i],
            recv_sem=pgr_sem.at[i],
            device_id=(p, pair),
            device_id_type=MESH,
        )

    def pair_block_send(j):
        part = (pl.ds(eager, steps - eager), slice(None), pl.ds(j * block_w, block_w))
        return pltpu.make_async_remote_copy(
            src_ref=gp.at[part],
            dst_ref=pair_gp.at[part],
            send_sem=pbs_sem.at[j],
            recv_sem=pbr_sem.at[j],
            device_id=(p, pair),
            device_id_type=MESH,
        )

    def middle_copy(k, j):
        return pltpu.make_async_remote_copy(
            src_ref=rs_send.at[k, j],
            dst_ref=rs_recv.at[k, j],
            send_sem=rss_sem.at[k, j],
            recv_sem=rsr_sem.at[k, j],
            device_id=(p, middle),
            device_id_type=MESH,
        )

    def tail_copy(j):
        return pltpu.make_async_remote_copy(
            src_ref=tail_send.at[j],
            dst_ref=tail_recv.at[j],
            send_sem=ts_sem.at[j],
            recv_sem=tr_sem.at[j],
            device_id=(p, pair),
            device_id_type=MESH,
        )

    def keep(source, target, sem, i):
        return pltpu.make_async_copy(source.at[i], target.at[0, i - micro], sem.at[i])

    @pl.when(p == 0)
    def _():
        load(down_in, vin.at[pl.ds(0, micro)], 0).wait()
        load(up_in, vin.at[pl.ds(micro, micro)], 1).wait()

    load(weight_hbm.at[0], weight, 4).wait()
    pl.semaphore_wait(barrier, 5)

    def transpose_weight():
        def strip(j, carry):
            rows_of = pl.ds(pl.multiple_of(j * 128, 128), 128)
            for k in range(width // 256):
                cols = slice(k * 256, (k + 1) * 256)
                weight_t[cols, rows_of] = weight[rows_of, cols].T
            return carry

        lax.fori_loop(0, width // 128, strip, 0)

    @pl.when(p >= sections // 2)
    def _():
        transpose_weight()

    def forward(i):
        @pl.when(p > 0)
        def _():
            for t in range(tiles):
                forward_send(i, t).wait_recv()

        v = vin[i].astype(F32)
        s = lax.rsqrt(jnp.mean(v * v, axis=-1, keepdims=True) + NORM_EPS)
        hidden = (v * s).astype(BF16)
        hid[i] = hidden
        inv[i] = jnp.broadcast_to(s, (rows, 128))
        for t in range(tiles):
            cols = slice(t * tile, (t + 1) * tile)
            pre = jnp.dot(hidden, weight[:, cols], preferred_element_type=F32)
            sigma = 1.0 / (1.0 + jnp.exp(-pre))
            y[i, :, cols] = (vin[i, :, cols].astype(F32) + pre * sigma).astype(BF16)

            @pl.when(p < last)
            def _():
                forward_send(i, t).start()

            slope[i, :, cols] = sigma * (1.0 + pre * (1.0 - sigma))

        @pl.when(i >= micro)
        def _():
            keep(y, out, oms_sem, i).start()

    def transpose_hidden():
        per = 128 // rows
        for j in range(steps // per):
            block = hid[j * per : (j + 1) * per].reshape(per * rows, width)
            hid_t[:, j * 128 : (j + 1) * 128] = block.T

    @pl.when(p == last)
    def _():
        load(down_ct, gin.at[pl.ds(0, micro)], 2).wait()
        load(up_ct, gin.at[pl.ds(micro, micro)], 3).wait()

    def backward(i):
        @pl.when(p < last)
        def _():
            backward_send(i).wait_recv()

        g = gin[i].astype(F32)
        grad_pre = (g * slope[i]).astype(BF16)
        gp[i] = grad_pre
        if line:

            @pl.when(jnp.logical_and(is_end, i < eager))
            def _():
                pair_gp_send(i).start()

            @pl.when(jnp.logical_and(is_end, i == steps - 1))
            def _():
                for j in range(blocks):
                    pair_block_send(j).start()

        dots = jnp.zeros((rows, 1), F32)
        for t in range(tiles):
            cols = slice(t * tile, (t + 1) * tile)
            part = jnp.dot(grad_pre, weight_t[:, cols], preferred_element_type=F32)
            gh[:, cols] = part
            dots += jnp.sum(part * vin[i, :, cols].astype(F32), axis=-1, keepdims=True)
        s = inv[i][:, :1]
        factor = s * s * (dots * (1.0 / width))
        for t in range(tiles):
            cols = slice(t * tile, (t + 1) * tile)
            v = vin[i, :, cols].astype(F32)
            gout[i, :, cols] = (
                gin[i, :, cols].astype(F32) + s * (gh[:, cols] - v * factor)
            ).astype(BF16)

        @pl.when(p > 0)
        def _():
            backward_send(i).start()

        @pl.when(i >= micro)
        def _():
            keep(gout, grads, gms_sem, i).start()

    lead = jnp.minimum(steps, LEAD * (last - p))

    def turn(t, carry):
        @pl.when(t < steps)
        def _():
            forward(t)

        @pl.when(t == steps - 1)
        def _():
            transpose_hidden()
            if line:

                @pl.when(is_end)
                def _():
                    pair_hid_send().start()

            @pl.when(p < sections // 2)
            def _():
                transpose_weight()


        @pl.when(t >= lead)
        def _():
            backward(t - lead)

        return carry

    lax.fori_loop(0, steps + lead, turn, 0)

    def piece(left, right, chunk, j):
        at = pl.multiple_of(chunk * chunk_rows, chunk_rows)
        return jnp.dot(
            left[pl.ds(at, chunk_rows), :],
            right[:, :, j * block_w : (j + 1) * block_w].reshape(steps * rows, block_w),
            preferred_element_type=F32,
        )

    def to_mirror(i, carry):
        mirror_send(y, out, oms_sem, omr_sem, i).start()
        mirror_send(gout, grads, gms_sem, gmr_sem, i).start()
        return carry

    if line:

        @pl.when(is_end)
        def _():
            lax.fori_loop(0, micro, to_mirror, 0)
            for j in range(blocks):
                cols = slice(j * block_w, (j + 1) * block_w)
                own = piece(hid_t, gp, z, j)
                tail_copy(j).wait_recv()
                wgrad[0, :, cols] = own + tail_recv[j].astype(F32)

        @pl.when(jnp.logical_not(is_end))
        def _():
            pair_hid_send().wait_recv()
            for i in range(eager):
                pair_gp_send(i).wait_recv()
            for j in range(blocks):
                pair_block_send(j).wait_recv()
                for k, chunk in enumerate((far, middle)):
                    total = piece(hid_t, gp, chunk, j) + piece(pair_hid, pair_gp, chunk, j)
                    rs_send[k, j] = total.astype(BF16)
                    middle_copy(k, j).start()
            lax.fori_loop(0, micro, to_mirror, 0)
            for j in range(blocks):
                cols = slice(j * block_w, (j + 1) * block_w)
                own = piece(hid_t, gp, pair, j)
                middle_copy(0, j).wait_recv()
                tail_send[j] = (own + rs_recv[0, j].astype(F32)).astype(BF16)
                tail_copy(j).start()
                own = piece(hid_t, gp, z, j) + piece(pair_hid, pair_gp, z, j)
                middle_copy(1, j).wait_recv()
                wgrad[0, :, cols] = own + rs_recv[1, j].astype(F32)

    else:

        def ring_send(s, j, way):
            return pltpu.make_async_remote_copy(
                src_ref=rs_send.at[s, j],
                dst_ref=rs_recv.at[s, j],
                send_sem=rss_sem.at[s, j],
                recv_sem=rsr_sem.at[s, j],
                device_id=(p, z_next if way > 0 else z_prev),
                device_id_type=MESH,
            )

        order = []
        for j in range(blocks // 2):
            order += [(j, 1), (blocks // 2 + j, -1)]

        for j, way in order:
            chunk = lax.rem(z - way + replicas, replicas)
            rs_send[0, j] = piece(hid_t, gp, chunk, j).astype(BF16)
            ring_send(0, j, way).start()

        lax.fori_loop(0, micro, to_mirror, 0)

        def ring(s, carry):
            for j, way in order:
                chunk = lax.rem(z - way * (1 + s) + replicas, replicas)
                own = piece(hid_t, gp, chunk, j)
                ring_send(s - 1, j, way).wait_recv()
                rs_send[s, j] = (own + rs_recv[s - 1, j].astype(F32)).astype(BF16)
                ring_send(s, j, way).start()
            return carry

        lax.fori_loop(1, replicas - 1, ring, 0)

        for j, way in order:
            cols = slice(j * block_w, (j + 1) * block_w)
            own = piece(hid_t, gp, z, j)
            ring_send(replicas - 2, j, way).wait_recv()
            wgrad[0, :, cols] = own + rs_recv[replicas - 2, j].astype(F32)

    def drain(i, carry):
        @pl.when(p < last)
        def _():
            for t in range(tiles):
                forward_send(i, t).wait_send()

        @pl.when(p > 0)
        def _():
            backward_send(i).wait_send()

        @pl.when(i < micro)
        def _():
            mirror_send(y, out, oms_sem, omr_sem, i).wait()
            mirror_send(gout, grads, gms_sem, gmr_sem, i).wait()

        @pl.when(i >= micro)
        def _():
            keep(y, out, oms_sem, i).wait()
            keep(gout, grads, gms_sem, i).wait()

        return carry

    lax.fori_loop(0, steps, drain, 0)

    if line:

        @pl.when(is_end)
        def _():
            pair_hid_send().wait_send()
            for i in range(eager):
                pair_gp_send(i).wait_send()
            for j in range(blocks):
                pair_block_send(j).wait_send()

        @pl.when(jnp.logical_not(is_end))
        def _():
            for j in range(blocks):
                middle_copy(0, j).wait_send()
                middle_copy(1, j).wait_send()
                tail_copy(j).wait_send()

    else:

        def ring_drain(s, carry):
            for j, way in order:
                ring_send(s, j, way).wait_send()
            return carry

        lax.fori_loop(0, replicas - 1, ring_drain, 0)


def local(up_input, down_input, up_cotangent, down_cotangent, weights):
    sections = lax.axis_size("pipe")
    replicas = lax.axis_size("dp")
    micro, rows, width = up_input.shape
    steps = 2 * micro
    chunk_rows = width // replicas
    line = replicas == 4
    blocks = 6 if line and width % 768 == 0 else 4
    hops = 2 if line else replicas - 1
    tiles = width // 512 if width % 512 == 0 else 1
    block_w = width // blocks
    acts = (steps, rows, width)
    anywhere = pl.BlockSpec(memory_space=pltpu.HBM)
    vmem = pl.BlockSpec(memory_space=pltpu.VMEM)
    dma = pltpu.SemaphoreType.DMA
    flops = 6 * steps * rows * width * width
    outs, grads, wgrad = pl.pallas_call(
        functools.partial(window_kernel, sections, replicas),
        out_shape=(
            jax.ShapeDtypeStruct((2, micro, rows, width), BF16),
            jax.ShapeDtypeStruct((2, micro, rows, width), BF16),
            jax.ShapeDtypeStruct((1, chunk_rows, width), F32),
        ),
        in_specs=[anywhere] * 5,
        out_specs=(anywhere, anywhere, vmem),
        scratch_shapes=[
            pltpu.VMEM((width, width), BF16),
            pltpu.VMEM((width, width), BF16),
            pltpu.VMEM(acts, BF16),
            pltpu.VMEM(acts, BF16),
            pltpu.VMEM(acts, BF16),
            pltpu.VMEM((width, steps * rows), BF16),
            pltpu.VMEM(acts, F32),
            pltpu.VMEM((steps, rows, 128), F32),
            pltpu.VMEM(acts, BF16),
            pltpu.VMEM(acts, BF16),
            pltpu.VMEM(acts, BF16),
            pltpu.VMEM((rows, width), F32),
            pltpu.VMEM((hops, blocks, chunk_rows, block_w), BF16),
            pltpu.VMEM((hops, blocks, chunk_rows, block_w), BF16),
            pltpu.VMEM((blocks, chunk_rows, block_w), BF16),
            pltpu.VMEM((blocks, chunk_rows, block_w), BF16),
            pltpu.VMEM((width, steps * rows), BF16),
            pltpu.VMEM(acts, BF16),
            dma((5,)),
            dma((steps, tiles)),
            dma((steps, tiles)),
            dma((steps,)),
            dma((steps,)),
            dma((steps,)),
            dma((steps,)),
            dma((steps,)),
            dma((steps,)),
            dma((hops, blocks)),
            dma((hops, blocks)),
            dma((blocks,)),
            dma((blocks,)),
            dma((1,)),
            dma((1,)),
            dma((steps,)),
            dma((steps,)),
            dma((blocks,)),
            dma((blocks,)),
        ],
        compiler_params=pltpu.CompilerParams(
            collective_id=0, has_side_effects=True, vmem_limit_bytes=63 * 1024 * 1024
        ),
        cost_estimate=pl.CostEstimate(
            flops=flops, bytes_accessed=20 * 1024 * 1024, transcendentals=steps * rows * width
        ),
    )(up_input, down_input, up_cotangent, down_cotangent, weights)
    return (outs[:, None], grads[:, None], wgrad)


def solution(mesh):
    return jax.shard_map(
        local,
        mesh=mesh,
        in_specs=(
            P(None, "dp", None),
            P(None, "dp", None),
            P(None, "dp", None),
            P(None, "dp", None),
            P("pipe", None, None),
        ),
        out_specs=(
            P(None, "pipe", None, "dp", None),
            P(None, "pipe", None, "dp", None),
            P("pipe", "dp", None),
        ),
        check_vma=False,
    )
```

```python
import functools

import jax
import jax.numpy as jnp
from jax import lax
from jax.experimental import pallas as pl
from jax.experimental.pallas import tpu as pltpu
from jax.sharding import PartitionSpec as P

NORM_EPS = 1e-06
LEAD = 4
MESH = pl.DeviceIdType.MESH
F32 = jnp.float32
BF16 = jnp.bfloat16


def window_kernel(
    sections,
    replicas,
    up_in,
    down_in,
    up_ct,
    down_ct,
    weight_hbm,
    out,
    grads,
    wgrad,
    weight,
    weight_t,
    vin,
    y,
    hid,
    hid_t,
    slope,
    inv,
    gin,
    gp,
    gout,
    gh,
    rs_send,
    rs_recv,
    tail_send,
    tail_recv,
    pair_hid,
    pair_gp,
    load_sem,
    fs_sem,
    fr_sem,
    bs_sem,
    br_sem,
    oms_sem,
    omr_sem,
    gms_sem,
    gmr_sem,
    rss_sem,
    rsr_sem,
    ts_sem,
    tr_sem,
    phs_sem,
    phr_sem,
    pgs_sem,
    pgr_sem,
    pbs_sem,
    pbr_sem,
):
    p = lax.axis_index("pipe")
    z = lax.axis_index("dp")
    steps, rows, width = vin.shape
    micro = steps // 2
    last = sections - 1
    after = lax.rem(p + 1, sections)
    before = lax.rem(p + sections - 1, sections)
    mirror = last - p
    z_next = lax.rem(z + 1, replicas)
    z_prev = lax.rem(z + replicas - 1, replicas)
    tile = 512 if width % 512 == 0 else width
    tiles = width // tile
    blocks = rs_send.shape[1]
    block_w = width // blocks
    chunk_rows = width // replicas

    barrier = pltpu.get_barrier_semaphore()
    for peer in ((after, z), (before, z), (mirror, z), (p, z_next), (p, z_prev)):
        pl.semaphore_signal(barrier, inc=1, device_id=peer, device_id_type=MESH)

    def load(source, target, index):
        return pltpu.make_async_copy(source, target, load_sem.at[index])

    load(weight_hbm.at[0], weight, 4).start()

    @pl.when(p == 0)
    def _():
        load(down_in, vin.at[pl.ds(0, micro)], 0).start()
        load(up_in, vin.at[pl.ds(micro, micro)], 1).start()

    @pl.when(p == last)
    def _():
        load(down_ct, gin.at[pl.ds(0, micro)], 2).start()
        load(up_ct, gin.at[pl.ds(micro, micro)], 3).start()

    def forward_send(i, t):
        part = pl.ds(t * tile, tile)
        return pltpu.make_async_remote_copy(
            src_ref=y.at[i, :, part],
            dst_ref=vin.at[i, :, part],
            send_sem=fs_sem.at[i, t],
            recv_sem=fr_sem.at[i, t],
            device_id=(after, z),
            device_id_type=MESH,
        )

    def backward_send(i):
        return pltpu.make_async_remote_copy(
            src_ref=gout.at[i],
            dst_ref=gin.at[i],
            send_sem=bs_sem.at[i],
            recv_sem=br_sem.at[i],
            device_id=(before, z),
            device_id_type=MESH,
        )

    def mirror_send(source, target, send_sem, recv_sem, i):
        return pltpu.make_async_remote_copy(
            src_ref=source.at[i],
            dst_ref=target.at[1, i],
            send_sem=send_sem.at[i],
            recv_sem=recv_sem.at[i],
            device_id=(mirror, z),
            device_id_type=MESH,
        )

    line = replicas == 4
    eager = steps - 2
    is_end = jnp.logical_or(z == 0, z == replicas - 1)
    pair = z + 1 - 2 * lax.rem(z, 2)
    middle = jnp.where(z == 1, 2, 1)
    far = jnp.where(z == 1, 3, 0)
    kept = width - chunk_rows

    def pair_hid_send():
        part = pl.ds(pl.multiple_of(jnp.where(z == 0, chunk_rows, 0), chunk_rows), kept)
        return pltpu.make_async_remote_copy(
            src_ref=hid_t.at[part],
            dst_ref=pair_hid.at[part],
            send_sem=phs_sem.at[0],
            recv_sem=phr_sem.at[0],
            device_id=(p, pair),
            device_id_type=MESH,
        )

    def pair_gp_send(i):
        return pltpu.make_async_remote_copy(
            src_ref=gp.at[i],
            dst_ref=pair_gp.at[i],
            send_sem=pgs_sem.at[i],
            recv_sem=pgr_sem.at[i],
            device_id=(p, pair),
            device_id_type=MESH,
        )

    def pair_block_send(j):
        part = (pl.ds(eager, steps - eager), slice(None), pl.ds(j * block_w, block_w))
        return pltpu.make_async_remote_copy(
            src_ref=gp.at[part],
            dst_ref=pair_gp.at[part],
            send_sem=pbs_sem.at[j],
            recv_sem=pbr_sem.at[j],
            device_id=(p, pair),
            device_id_type=MESH,
        )

    def middle_copy(k, j):
        return pltpu.make_async_remote_copy(
            src_ref=rs_send.at[k, j],
            dst_ref=rs_recv.at[k, j],
            send_sem=rss_sem.at[k, j],
            recv_sem=rsr_sem.at[k, j],
            device_id=(p, middle),
            device_id_type=MESH,
        )

    def tail_copy(j):
        return pltpu.make_async_remote_copy(
            src_ref=tail_send.at[j],
            dst_ref=tail_recv.at[j],
            send_sem=ts_sem.at[j],
            recv_sem=tr_sem.at[j],
            device_id=(p, pair),
            device_id_type=MESH,
        )

    def keep(source, target, sem, i):
        return pltpu.make_async_copy(source.at[i], target.at[0, i - micro], sem.at[i])

    @pl.when(p == 0)
    def _():
        load(down_in, vin.at[pl.ds(0, micro)], 0).wait()
        load(up_in, vin.at[pl.ds(micro, micro)], 1).wait()

    load(weight_hbm.at[0], weight, 4).wait()
    def transpose_weight():
        def strip(j, carry):
            rows_of = pl.ds(pl.multiple_of(j * 128, 128), 128)
            for k in range(width // 256):
                cols = slice(k * 256, (k + 1) * 256)
                weight_t[cols, rows_of] = weight[rows_of, cols].T
            return carry

        lax.fori_loop(0, width // 128, strip, 0)

    @pl.when(p >= sections // 2)
    def _():
        transpose_weight()

    pl.semaphore_wait(barrier, 5)

    def forward(i):
        @pl.when(p > 0)
        def _():
            for t in range(tiles):
                forward_send(i, t).wait_recv()

        v = vin[i].astype(F32)
        s = lax.rsqrt(jnp.mean(v * v, axis=-1, keepdims=True) + NORM_EPS)
        hidden = (v * s).astype(BF16)
        hid[i] = hidden
        inv[i] = jnp.broadcast_to(s, (rows, 128))
        for t in range(tiles):
            cols = slice(t * tile, (t + 1) * tile)
            pre = jnp.dot(hidden, weight[:, cols], preferred_element_type=F32)
            sigma = 1.0 / (1.0 + jnp.exp(-pre))
            y[i, :, cols] = (vin[i, :, cols].astype(F32) + pre * sigma).astype(BF16)

            @pl.when(p < last)
            def _():
                forward_send(i, t).start()

            slope[i, :, cols] = sigma * (1.0 + pre * (1.0 - sigma))

        @pl.when(i >= micro)
        def _():
            keep(y, out, oms_sem, i).start()

    def transpose_hidden():
        per = 128 // rows
        for j in range(steps // per):
            block = hid[j * per : (j + 1) * per].reshape(per * rows, width)
            hid_t[:, j * 128 : (j + 1) * 128] = block.T

    @pl.when(p == last)
    def _():
        load(down_ct, gin.at[pl.ds(0, micro)], 2).wait()
        load(up_ct, gin.at[pl.ds(micro, micro)], 3).wait()

    def backward(i):
        @pl.when(p < last)
        def _():
            backward_send(i).wait_recv()

        g = gin[i].astype(F32)
        grad_pre = (g * slope[i]).astype(BF16)
        gp[i] = grad_pre
        if line:

            @pl.when(jnp.logical_and(is_end, i < eager))
            def _():
                pair_gp_send(i).start()

            @pl.when(jnp.logical_and(is_end, i == steps - 1))
            def _():
                for j in range(blocks):
                    pair_block_send(j).start()

        dots = jnp.zeros((rows, 1), F32)
        for t in range(tiles):
            cols = slice(t * tile, (t + 1) * tile)
            part = jnp.dot(grad_pre, weight_t[:, cols], preferred_element_type=F32)
            gh[:, cols] = part
            dots += jnp.sum(part * vin[i, :, cols].astype(F32), axis=-1, keepdims=True)
        s = inv[i][:, :1]
        factor = s * s * (dots * (1.0 / width))
        for t in range(tiles):
            cols = slice(t * tile, (t + 1) * tile)
            v = vin[i, :, cols].astype(F32)
            gout[i, :, cols] = (
                gin[i, :, cols].astype(F32) + s * (gh[:, cols] - v * factor)
            ).astype(BF16)

        @pl.when(p > 0)
        def _():
            backward_send(i).start()

        @pl.when(i >= micro)
        def _():
            keep(gout, grads, gms_sem, i).start()

    lead = jnp.minimum(steps, LEAD * (last - p))

    def turn(t, carry):
        @pl.when(t < steps)
        def _():
            forward(t)

        @pl.when(t == steps - 1)
        def _():
            transpose_hidden()
            if line:

                @pl.when(is_end)
                def _():
                    pair_hid_send().start()

            @pl.when(p < sections // 2)
            def _():
                transpose_weight()


        @pl.when(t >= lead)
        def _():
            backward(t - lead)

        return carry

    lax.fori_loop(0, steps + lead, turn, 0)

    def piece(left, right, chunk, j):
        at = pl.multiple_of(chunk * chunk_rows, chunk_rows)
        return jnp.dot(
            left[pl.ds(at, chunk_rows), :],
            right[:, :, j * block_w : (j + 1) * block_w].reshape(steps * rows, block_w),
            preferred_element_type=F32,
        )

    def to_mirror(i, carry):
        mirror_send(y, out, oms_sem, omr_sem, i).start()
        mirror_send(gout, grads, gms_sem, gmr_sem, i).start()
        return carry

    if line:

        @pl.when(is_end)
        def _():
            lax.fori_loop(0, micro, to_mirror, 0)
            for j in range(blocks):
                cols = slice(j * block_w, (j + 1) * block_w)
                own = piece(hid_t, gp, z, j)
                tail_copy(j).wait_recv()
                wgrad[0, :, cols] = own + tail_recv[j].astype(F32)

        @pl.when(jnp.logical_not(is_end))
        def _():
            pair_hid_send().wait_recv()
            for i in range(eager):
                pair_gp_send(i).wait_recv()
            for j in range(blocks):
                pair_block_send(j).wait_recv()
                for k, chunk in enumerate((far, middle)):
                    total = piece(hid_t, gp, chunk, j) + piece(pair_hid, pair_gp, chunk, j)
                    rs_send[k, j] = total.astype(BF16)
                    middle_copy(k, j).start()
            lax.fori_loop(0, micro, to_mirror, 0)
            for j in range(blocks):
                cols = slice(j * block_w, (j + 1) * block_w)
                own = piece(hid_t, gp, pair, j)
                middle_copy(0, j).wait_recv()
                tail_send[j] = (own + rs_recv[0, j].astype(F32)).astype(BF16)
                tail_copy(j).start()
                own = piece(hid_t, gp, z, j) + piece(pair_hid, pair_gp, z, j)
                middle_copy(1, j).wait_recv()
                wgrad[0, :, cols] = own + rs_recv[1, j].astype(F32)

    else:

        def ring_send(s, j, way):
            return pltpu.make_async_remote_copy(
                src_ref=rs_send.at[s, j],
                dst_ref=rs_recv.at[s, j],
                send_sem=rss_sem.at[s, j],
                recv_sem=rsr_sem.at[s, j],
                device_id=(p, z_next if way > 0 else z_prev),
                device_id_type=MESH,
            )

        order = []
        for j in range(blocks // 2):
            order += [(j, 1), (blocks // 2 + j, -1)]

        for j, way in order:
            chunk = lax.rem(z - way + replicas, replicas)
            rs_send[0, j] = piece(hid_t, gp, chunk, j).astype(BF16)
            ring_send(0, j, way).start()

        lax.fori_loop(0, micro, to_mirror, 0)

        def ring(s, carry):
            for j, way in order:
                chunk = lax.rem(z - way * (1 + s) + replicas, replicas)
                own = piece(hid_t, gp, chunk, j)
                ring_send(s - 1, j, way).wait_recv()
                rs_send[s, j] = (own + rs_recv[s - 1, j].astype(F32)).astype(BF16)
                ring_send(s, j, way).start()
            return carry

        lax.fori_loop(1, replicas - 1, ring, 0)

        for j, way in order:
            cols = slice(j * block_w, (j + 1) * block_w)
            own = piece(hid_t, gp, z, j)
            ring_send(replicas - 2, j, way).wait_recv()
            wgrad[0, :, cols] = own + rs_recv[replicas - 2, j].astype(F32)

    def drain(i, carry):
        @pl.when(p < last)
        def _():
            for t in range(tiles):
                forward_send(i, t).wait_send()

        @pl.when(p > 0)
        def _():
            backward_send(i).wait_send()

        @pl.when(i < micro)
        def _():
            mirror_send(y, out, oms_sem, omr_sem, i).wait()
            mirror_send(gout, grads, gms_sem, gmr_sem, i).wait()

        @pl.when(i >= micro)
        def _():
            keep(y, out, oms_sem, i).wait()
            keep(gout, grads, gms_sem, i).wait()

        return carry

    lax.fori_loop(0, steps, drain, 0)

    if line:

        @pl.when(is_end)
        def _():
            pair_hid_send().wait_send()
            for i in range(eager):
                pair_gp_send(i).wait_send()
            for j in range(blocks):
                pair_block_send(j).wait_send()

        @pl.when(jnp.logical_not(is_end))
        def _():
            for j in range(blocks):
                middle_copy(0, j).wait_send()
                middle_copy(1, j).wait_send()
                tail_copy(j).wait_send()

    else:

        def ring_drain(s, carry):
            for j, way in order:
                ring_send(s, j, way).wait_send()
            return carry

        lax.fori_loop(0, replicas - 1, ring_drain, 0)


def local(up_input, down_input, up_cotangent, down_cotangent, weights):
    sections = lax.axis_size("pipe")
    replicas = lax.axis_size("dp")
    micro, rows, width = up_input.shape
    steps = 2 * micro
    chunk_rows = width // replicas
    line = replicas == 4
    blocks = 6 if line and width % 768 == 0 else 4
    hops = 2 if line else replicas - 1
    tiles = width // 512 if width % 512 == 0 else 1
    block_w = width // blocks
    acts = (steps, rows, width)
    anywhere = pl.BlockSpec(memory_space=pltpu.HBM)
    vmem = pl.BlockSpec(memory_space=pltpu.VMEM)
    dma = pltpu.SemaphoreType.DMA
    flops = 6 * steps * rows * width * width
    outs, grads, wgrad = pl.pallas_call(
        functools.partial(window_kernel, sections, replicas),
        out_shape=(
            jax.ShapeDtypeStruct((2, micro, rows, width), BF16),
            jax.ShapeDtypeStruct((2, micro, rows, width), BF16),
            jax.ShapeDtypeStruct((1, chunk_rows, width), F32),
        ),
        in_specs=[anywhere] * 5,
        out_specs=(anywhere, anywhere, vmem),
        scratch_shapes=[
            pltpu.VMEM((width, width), BF16),
            pltpu.VMEM((width, width), BF16),
            pltpu.VMEM(acts, BF16),
            pltpu.VMEM(acts, BF16),
            pltpu.VMEM(acts, BF16),
            pltpu.VMEM((width, steps * rows), BF16),
            pltpu.VMEM(acts, F32),
            pltpu.VMEM((steps, rows, 128), F32),
            pltpu.VMEM(acts, BF16),
            pltpu.VMEM(acts, BF16),
            pltpu.VMEM(acts, BF16),
            pltpu.VMEM((rows, width), F32),
            pltpu.VMEM((hops, blocks, chunk_rows, block_w), BF16),
            pltpu.VMEM((hops, blocks, chunk_rows, block_w), BF16),
            pltpu.VMEM((blocks, chunk_rows, block_w), BF16),
            pltpu.VMEM((blocks, chunk_rows, block_w), BF16),
            pltpu.VMEM((width, steps * rows), BF16),
            pltpu.VMEM(acts, BF16),
            dma((5,)),
            dma((steps, tiles)),
            dma((steps, tiles)),
            dma((steps,)),
            dma((steps,)),
            dma((steps,)),
            dma((steps,)),
            dma((steps,)),
            dma((steps,)),
            dma((hops, blocks)),
            dma((hops, blocks)),
            dma((blocks,)),
            dma((blocks,)),
            dma((1,)),
            dma((1,)),
            dma((steps,)),
            dma((steps,)),
            dma((blocks,)),
            dma((blocks,)),
        ],
        compiler_params=pltpu.CompilerParams(
            collective_id=0, has_side_effects=True, vmem_limit_bytes=63 * 1024 * 1024
        ),
        cost_estimate=pl.CostEstimate(
            flops=flops, bytes_accessed=20 * 1024 * 1024, transcendentals=steps * rows * width
        ),
    )(up_input, down_input, up_cotangent, down_cotangent, weights)
    return (outs[:, None], grads[:, None], wgrad)


def solution(mesh):
    return jax.shard_map(
        local,
        mesh=mesh,
        in_specs=(
            P(None, "dp", None),
            P(None, "dp", None),
            P(None, "dp", None),
            P(None, "dp", None),
            P("pipe", None, None),
        ),
        out_specs=(
            P(None, "pipe", None, "dp", None),
            P(None, "pipe", None, "dp", None),
            P("pipe", "dp", None),
        ),
        check_vma=False,
    )
```
